32 devices in a mesh: grp: 1, mem: 32 (over z, y, x, core).
Axes of the slice: x: 2, y: 2, z: 4, core: 2. Of those that a mesh axis runs over, the one named last changes fastest.
Arguments:
- amplitudes: float32 [192, 1, 32, 2000], P('mem', 'grp'), may hold values from -6 to 6
- singles: float32 [250, 2000], replicated, may hold values from -5 to 5
- pair_list: int32 [192, 2], replicated, may hold values from 0 to 249, as said below
- mirror: int32 [192], replicated, may hold values from 0 to 191, as said below
- slab_rows: int32 [2048, 2], P('grp'), may hold values from 0 to 1999
- occ_energy: float32 [250], replicated, may hold values from -1 to -0.2
- vir_energy: float32 [2000], replicated, may hold values from 0.2 to 1
- integrals: float32 [2048, 1, 32, 2000], P('grp', None, 'mem'), may hold values from -0.0234375 to 0.0234375
Outputs:
- update: float32 [192, 2048], P('mem', 'grp')
The draws below stay inside these ranges and needn't reach their ends.
Inputs may be any that keep to these rules, and one draw needn't show every extreme that they name: `pair_list`: each row holds two occupied orbitals i < j; no pair appears twice. mirror[mirror[p]] = p and mirror[p] != p; a pair p of owner block k = p // 6 is mapped into owner block (k + 32 / 2) mod 32.
All inputs are finite; a program needn't handle non-finite values.
Results may differ from the reference program's by a relative error of at most 0.000073.
Values sent between devices are 32-bit elements; how exact they have to be, the bound alone decides.
A program may use at most 128 MiB of HBM per device.

```python
import jax
import jax.numpy as jnp
from jax import lax

NO = 250
NV = 2000
AB = 2048
PAIR_DEV = 6
CBQ = 32
PAIRS = 192
N_GRP = 1
N_MEM = 32


def draw_pair_list(key, part):
    pair_codes = jax.random.permutation(key, NO * NO)
    first_orb = pair_codes // NO
    second_orb = pair_codes % NO
    ranking = jnp.argsort((first_orb >= second_orb).astype(jnp.int32), stable=True)
    chosen = pair_codes[ranking[:PAIRS]]
    return jnp.stack([chosen // NO, chosen % NO], axis=1).astype(jnp.int32)


def draw_mirror(key, part):
    half_owners = N_MEM // 2
    owner_keys = jax.random.split(jax.random.fold_in(key, 17), half_owners)
    slot_perms = jax.vmap(lambda one_key: jax.random.permutation(one_key, PAIR_DEV))(owner_keys)
    inverse = jnp.argsort(slot_perms, axis=1)
    owner_ids = jnp.arange(half_owners, dtype=jnp.int32)[:, None]
    lower = (owner_ids + half_owners) * PAIR_DEV + slot_perms
    upper = owner_ids * PAIR_DEV + inverse
    return jnp.concatenate([lower.reshape(-1), upper.reshape(-1)]).astype(jnp.int32)


def place_ends(entries, key, smallest, largest):
    extent = entries.shape
    index_at = [jax.random.randint(jax.random.fold_in(key, axis), (), 0, extent[axis]) for axis in range(len(extent))]
    entries = entries.at[tuple(index_at)].set(smallest)
    longest = extent.index(max(extent))
    index_at[longest] = (index_at[longest] + 1) % extent[longest]
    return entries.at[tuple(index_at)].set(largest)


def steps_of(own_key, shape, cuts, least, high):
    factor_of = 1.0
    for dim, blocks in cuts:
        draws = jax.random.uniform(jax.random.fold_in(jax.random.fold_in(own_key, 6), dim), (blocks,), jnp.float32, least / len(cuts), high / len(cuts))
        factor_of = factor_of * jnp.repeat(jnp.exp(draws), shape[dim] // blocks).reshape((-1,) + (1,) * (len(shape) - 1 - dim))
    return factor_of


def noise(rng, dims, width, most, pieces=(), held_as=jnp.bfloat16):
    result = jax.random.normal(rng, dims, jnp.float32) * width
    if len(pieces) > 0:
        result = steps_of(rng, dims, pieces, -0.22, 0.18) * result
    return jnp.clip(result, min=-most, max=most).astype(held_as)


def setup_inputs(seed: int = 0) -> dict:
    splits = jax.random.split(jax.random.key(seed), 9)
    amplitudes = noise(splits[0], (PAIRS, N_GRP, CBQ, NV), 1.0, 6.0, ((0, 32),), jnp.float32)
    singles = noise(splits[1], (NO, NV), 0.8, 5.0, (), jnp.float32)
    pair_list = draw_pair_list(jax.random.fold_in(splits[8], 71), 0)
    mirror = draw_mirror(jax.random.fold_in(splits[8], 71), 0)
    slab_rows = place_ends(jax.random.randint(splits[4], (AB, 2), 0, NV), jax.random.fold_in(splits[4], 1), 0, NV - 1).astype(jnp.int32)
    occ_energy = jnp.clip(jax.random.uniform(splits[5], (NO,), jnp.float32, -1.0, -0.2), -1.0, -0.2)
    vir_energy = jnp.clip(jax.random.uniform(splits[6], (NV,), jnp.float32, 0.2, 1.0), 0.2, 1.0)
    integrals = noise(splits[7], (AB, N_GRP, CBQ, NV), (N_GRP * CBQ * NV) ** -0.5, 0.0234375, ((2, 32),), jnp.float32)
    return dict(amplitudes=amplitudes, singles=singles, pair_list=pair_list, mirror=mirror, slab_rows=slab_rows, occ_energy=occ_energy, vir_energy=vir_energy, integrals=integrals)


def reference(amplitudes, singles, pair_list, mirror, slab_rows, occ_energy, vir_energy, integrals):
    pair_total = amplitudes.shape[0]
    window_c = N_GRP * CBQ
    blocks = amplitudes.reshape(pair_total, window_c, NV)
    unpacked = blocks - jnp.take(blocks, mirror, axis=0)
    first_rows = jnp.take(singles, pair_list[:, 0], axis=0)
    second_rows = jnp.take(singles, pair_list[:, 1], axis=0)
    tau_full = unpacked + first_rows[:, :window_c, None] * second_rows[:, None, :] - second_rows[:, :window_c, None] * first_rows[:, None, :]
    flat_ints = integrals.reshape(integrals.shape[0], -1)
    ladder = 0.5 * lax.dot_general(tau_full.reshape(pair_total, -1), flat_ints, (((1,), (1,)), ((), ())), precision=lax.Precision.HIGHEST, preferred_element_type=jnp.float32)
    vir_first = jnp.take(vir_energy, slab_rows[:, 0])
    vir_second = jnp.take(vir_energy, slab_rows[:, 1])
    occ_first = jnp.take(occ_energy, pair_list[:, 0])
    occ_second = jnp.take(occ_energy, pair_list[:, 1])
    denominator = vir_first[None, :] + vir_second[None, :] - occ_first[:, None] - occ_second[:, None]
    return ladder / denominator
```

```python
import functools

import jax
import jax.numpy as jnp
from jax import lax
from jax.experimental import pallas as pl
from jax.experimental.pallas import tpu as pltpu
from jax.sharding import PartitionSpec as P

F32 = jnp.float32
BF16 = jnp.bfloat16
LANES = 128
CHUNKS = 2
COLUMN_BLOCKS = 4
PLANE = 4
CORES = 2


def to(device):
    return dict(device_id={"mem": device}, device_id_type=pl.DeviceIdType.MESH)


def bf16_dot(left, right):
    return jnp.dot(left, right, preferred_element_type=F32)


def split_two(value):
    high = value.astype(BF16)
    return high, (value - high.astype(F32)).astype(BF16)


def ladder_kernel(
    n,
    amp_ref,
    mirror_ref,
    pair_ref,
    own_ref,
    slab_ref,
    occ_ref,
    vir_ref,
    singles_hbm,
    ints_hbm,
    out_ref,
    send,
    recv,
    singles_ref,
    ints_raw,
    ints_high,
    ints_low,
    spart,
    rows_ref,
    partial,
    got_core,
    got_plane,
    ready_depth,
    got_depth,
    denom_ref,
    local_sem,
    ints_sem,
    a2a_send,
    a2a_recv,
    core_send,
    core_recv,
    plane_send,
    plane_recv,
    depth_send,
    depth_recv,
):
    me = lax.axis_index("mem")
    pair_dev, _, nc, nv = amp_ref.shape
    pairs = pair_dev * n
    depth_n = n // (PLANE * CORES)
    slab = ints_raw.shape[1]
    width = slab // COLUMN_BLOCKS
    blocks = send.shape[1] // (n * pair_dev)
    per_copy = pair_dev * blocks
    chunk_d = blocks * LANES
    core = lax.rem(me, CORES)
    plane = lax.rem(me // CORES, PLANE)
    depth = me // (CORES * PLANE)

    barrier = pltpu.get_barrier_semaphore()

    @pl.loop(1, n)
    def _(step):
        pl.semaphore_signal(barrier, inc=1, **to(lax.rem(me + step, n)))

    load_singles = pltpu.make_async_copy(singles_hbm, singles_ref, local_sem.at[0])
    load_singles.start()
    piece = nv // ints_sem.shape[0]
    load_ints = []
    for b in range(ints_sem.shape[0]):
        rows = pl.ds(b * piece, piece)
        load_ints.append(
            pltpu.make_async_copy(ints_hbm.at[rows], ints_raw.at[rows], ints_sem.at[b])
        )
        load_ints[-1].start()

    def fill(chunk):
        for j in range(blocks):
            first = (chunk * blocks + j) * LANES
            have = min(LANES, nv - first)
            for p in range(pair_dev):
                if have > 0:
                    value = amp_ref[p, 0, :, first : first + have]
                    if have < LANES:
                        value = jnp.concatenate(
                            [value, jnp.zeros((nc, LANES - have), F32)], axis=1
                        )
                else:
                    value = jnp.zeros((nc, LANES), F32)
                send[chunk, pl.ds(p * blocks + j, nc, stride=per_copy), :] = value

    def block_copy(chunk, target):
        source = pl.ds(pl.multiple_of(target * per_copy, 8), per_copy)
        landing = pl.ds(pl.multiple_of(me * per_copy, 8), per_copy)
        return pltpu.make_async_remote_copy(
            src_ref=send.at[chunk, source],
            dst_ref=recv.at[chunk, landing],
            send_sem=a2a_send.at[chunk],
            recv_sem=a2a_recv.at[chunk],
            **to(target),
        )

    def start_chunk(chunk):
        @pl.loop(1, n)
        def _(step):
            block_copy(chunk, lax.rem(me + step, n)).start()

        mine = pl.ds(pl.multiple_of(me * per_copy, 8), per_copy)
        pltpu.make_async_copy(
            send.at[chunk, mine], recv.at[chunk, mine], a2a_recv.at[chunk]
        ).start()

    fill(0)
    pl.semaphore_wait(barrier, n - 1)
    start_chunk(0)
    for chunk in range(1, CHUNKS):
        fill(chunk)
        start_chunk(chunk)

    table_rows = vir_ref.shape[0]

    def vir_of(which):
        orbital = slab_ref[pl.ds(which, 1), :]
        lane = jnp.bitwise_and(orbital, LANES - 1)
        row = jnp.right_shift(orbital, 7)
        hot = (lax.broadcasted_iota(jnp.int32, (LANES, slab), 0) == lane).astype(F32)
        table = jnp.dot(
            vir_ref[...], hot, precision=lax.Precision.HIGHEST, preferred_element_type=F32
        )
        at_row = lax.broadcasted_iota(jnp.int32, (table_rows, slab), 0) == row
        return jnp.sum(jnp.where(at_row, table, 0.0), axis=0, keepdims=True)

    no = occ_ref.shape[1]
    own_iota = lax.broadcasted_iota(jnp.int32, (pair_dev, no), 1)

    def occ_of(which):
        hot = own_iota == own_ref[:, which : which + 1]
        return jnp.sum(jnp.where(hot, occ_ref[...], 0.0), axis=1, keepdims=True)

    denom_ref[...] = vir_of(0) + vir_of(1) - occ_of(0) - occ_of(1)

    load_singles.wait()
    column = singles_ref[pl.ds(me, 1), :]
    pair_iota = lax.broadcasted_iota(jnp.int32, (pairs, no), 1)
    hot_i = pair_iota == pair_ref[:, 0:1]
    hot_j = pair_iota == pair_ref[:, 1:2]
    first_window = jnp.sum(jnp.where(hot_i, column, 0.0), axis=1, keepdims=True)
    second_window = jnp.sum(jnp.where(hot_j, column, 0.0), axis=1, keepdims=True)
    weights = jnp.where(hot_j, first_window, 0.0) - jnp.where(hot_i, second_window, 0.0)
    for chunk in range(CHUNKS):
        first = chunk * chunk_d
        have = min(chunk_d, nv - first)
        value = lax.dot_general(
            weights,
            singles_ref[first : first + have, :],
            (((1,), (1,)), ((), ())),
            precision=lax.Precision.HIGHEST,
            preferred_element_type=F32,
        )
        if have < chunk_d:
            value = jnp.concatenate([value, jnp.zeros((pairs, chunk_d - have), F32)], axis=1)
        spart[chunk] = value

    for b in range(len(load_ints)):
        load_ints[b].wait()

        @pl.loop(0, piece // 16)
        def _(i):
            at = pl.ds(pl.multiple_of(b * piece + i * 16, 16), 16)
            high, low = split_two(ints_raw[at, :])
            ints_high[at, :] = high
            ints_low[at, :] = low

    padded = CHUNKS * chunk_d
    if padded > nv:
        ints_high[nv:padded, :] = jnp.zeros((padded - nv, slab), BF16)
        ints_low[nv:padded, :] = jnp.zeros((padded - nv, slab), BF16)

    pair_row = lax.broadcasted_iota(jnp.int32, (pairs, pairs), 0)
    slot = lax.rem(pair_row, pair_dev)
    rest = pair_row // pair_dev
    at_depth = lax.rem(rest, depth_n)
    rest = rest // depth_n
    pair_of_row = (at_depth * PLANE * CORES + lax.rem(rest, PLANE) * CORES + rest // PLANE) * pair_dev + slot
    pair_column = lax.broadcasted_iota(jnp.int32, (pairs, pairs), 1)
    unpack = (
        (pair_column == pair_of_row).astype(F32) - (pair_column == mirror_ref[...]).astype(F32)
    ).astype(BF16)

    half = pairs // CORES
    plane_rows = half // PLANE

    def tau_parts(chunk):
        whole = recv.at[chunk]
        pltpu.make_async_copy(whole, whole, a2a_recv.at[chunk]).wait()
        for j in range(blocks):
            rows_ref[:, j * LANES : (j + 1) * LANES] = recv[chunk, pl.ds(j, pairs, stride=blocks), :]
        value = rows_ref[...]
        one, two = split_two(value)
        three = (value - one.astype(F32) - two.astype(F32)).astype(BF16)
        tau = (bf16_dot(unpack, one) + bf16_dot(unpack, two)) + bf16_dot(unpack, three)
        return split_two(tau + spart[chunk])

    def product(chunk, parts, nb):
        high, low = parts
        at = pl.ds(chunk * chunk_d, chunk_d)
        columns = pl.ds(nb * width, width)
        right = ints_high[at, columns]
        value = bf16_dot(high, right) + bf16_dot(low, right)
        value = value + bf16_dot(high, ints_low[at, columns])
        return value.reshape(CORES, PLANE, plane_rows, width)

    for chunk in range(CHUNKS - 1):
        parts = tau_parts(chunk)
        for nb in range(COLUMN_BLOCKS):
            value = product(chunk, parts, nb)
            partial[nb] = value if chunk == 0 else partial[nb] + value
    parts = tau_parts(CHUNKS - 1)

    def core_copy(nb):
        return pltpu.make_async_remote_copy(
            src_ref=partial.at[nb, 1 - core],
            dst_ref=got_core.at[nb],
            send_sem=core_send.at[nb],
            recv_sem=core_recv.at[nb],
            **to(me + 1 - 2 * core),
        )

    def plane_copy(nb, step):
        other = lax.rem(plane + step, PLANE)
        return pltpu.make_async_remote_copy(
            src_ref=partial.at[nb, core, other],
            dst_ref=got_plane.at[nb, step - 1],
            send_sem=plane_send.at[nb, step - 1],
            recv_sem=plane_recv.at[nb, step - 1],
            **to((depth * PLANE + other) * CORES + core),
        )

    def depth_copy(nb, step):
        other = lax.rem(depth + step, depth_n)
        return pltpu.make_async_remote_copy(
            src_ref=ready_depth.at[nb, other],
            dst_ref=got_depth.at[nb, step - 1],
            send_sem=depth_send.at[nb, step - 1],
            recv_sem=depth_recv.at[nb, step - 1],
            **to((other * PLANE + plane) * CORES + core),
        )

    def contract(nb):
        value = product(CHUNKS - 1, parts, nb)
        partial[nb] = partial[nb] + value if CHUNKS > 1 else value
        core_copy(nb).start()

    def add_core(nb):
        core_copy(nb).wait_recv()
        partial[nb, core] = partial[nb, core] + got_core[nb]
        for step in range(1, PLANE):
            plane_copy(nb, step).start()

    def add_plane(nb):
        for step in range(1, PLANE):
            plane_copy(nb, step).wait_recv()
        value = partial[nb, core, plane]
        for step in range(1, PLANE):
            value = value + got_plane[nb, step - 1]
        for z in range(depth_n):
            ready_depth[nb, z] = value[z * pair_dev : (z + 1) * pair_dev]
        for step in range(1, depth_n):
            depth_copy(nb, step).start()

    def add_depth(nb):
        for step in range(1, depth_n):
            depth_copy(nb, step).wait_recv()
        value = ready_depth[nb, depth]
        for step in range(1, depth_n):
            value = value + got_depth[nb, step - 1]
        columns = slice(nb * width, (nb + 1) * width)
        out_ref[:, columns] = 0.5 * value / denom_ref[:, columns]

    for step in range(COLUMN_BLOCKS + 3):
        for lag, stage in enumerate((contract, add_core, add_plane, add_depth)):
            if 0 <= step - lag < COLUMN_BLOCKS:
                stage(step - lag)

    for nb in range(COLUMN_BLOCKS):
        core_copy(nb).wait_send()
        for step in range(1, PLANE):
            plane_copy(nb, step).wait_send()
        for step in range(1, depth_n):
            depth_copy(nb, step).wait_send()
    for chunk in range(CHUNKS):
        @pl.loop(1, n)
        def _(step):
            block_copy(chunk, lax.rem(me + step, n)).wait_send()


def kernel_body(n, amplitudes, singles, pair_list, mirror, slab_rows, occ_energy, vir_energy, integrals):
    pair_dev, _, nc, nv = amplitudes.shape
    slab = integrals.shape[0]
    no = singles.shape[0]
    pairs = pair_dev * n
    depth_n = n // (PLANE * CORES)
    member = lax.axis_index("mem")
    blocks = -(-nv // (LANES * CHUNKS))
    padded = blocks * CHUNKS * LANES
    width = slab // COLUMN_BLOCKS

    def in_row_order(values):
        cut = values.reshape(depth_n, PLANE, CORES, pair_dev, -1)
        return cut.transpose(2, 1, 0, 3, 4).reshape(pairs, -1)

    own = lax.dynamic_slice_in_dim(pair_list, member * pair_dev, pair_dev, 0)
    table = jnp.pad(vir_energy, (0, -nv % LANES)).reshape(-1, LANES)
    ints = jnp.transpose(integrals, (1, 2, 3, 0)).reshape(nv, slab)
    pieces = max(k for k in range(1, 9) if nv % (16 * k) == 0)
    vmem = pl.BlockSpec(memory_space=pltpu.VMEM)
    hbm = pl.BlockSpec(memory_space=pl.ANY)
    dma = pltpu.SemaphoreType.DMA
    plane_rows = pairs // (CORES * PLANE)
    return pl.pallas_call(
        functools.partial(ladder_kernel, n),
        out_shape=jax.ShapeDtypeStruct((pair_dev, slab), F32),
        in_specs=[vmem] * 7 + [hbm] * 2,
        out_specs=vmem,
        scratch_shapes=[
            pltpu.VMEM((CHUNKS, pairs * blocks, LANES), F32),
            pltpu.VMEM((CHUNKS, pairs * blocks, LANES), F32),
            pltpu.VMEM((nv, no), F32),
            pltpu.VMEM((nv, slab), F32),
            pltpu.VMEM((padded, slab), BF16),
            pltpu.VMEM((padded, slab), BF16),
            pltpu.VMEM((CHUNKS, pairs, blocks * LANES), F32),
            pltpu.VMEM((pairs, blocks * LANES), F32),
            pltpu.VMEM((COLUMN_BLOCKS, CORES, PLANE, plane_rows, width), F32),
            pltpu.VMEM((COLUMN_BLOCKS, PLANE, plane_rows, width), F32),
            pltpu.VMEM((COLUMN_BLOCKS, PLANE - 1, plane_rows, width), F32),
            pltpu.VMEM((COLUMN_BLOCKS, depth_n, pair_dev, width), F32),
            pltpu.VMEM((COLUMN_BLOCKS, depth_n - 1, pair_dev, width), F32),
            pltpu.VMEM((pair_dev, slab), F32),
            dma((1,)),
            dma((pieces,)),
            dma((CHUNKS,)),
            dma((CHUNKS,)),
            dma((COLUMN_BLOCKS,)),
            dma((COLUMN_BLOCKS,)),
            dma((COLUMN_BLOCKS, PLANE - 1)),
            dma((COLUMN_BLOCKS, PLANE - 1)),
            dma((COLUMN_BLOCKS, depth_n - 1)),
            dma((COLUMN_BLOCKS, depth_n - 1)),
        ],
        compiler_params=pltpu.CompilerParams(
            collective_id=0, has_side_effects=True, vmem_limit_bytes=58 * 2**20
        ),
    )(
        amplitudes,
        in_row_order(mirror),
        in_row_order(pair_list),
        own,
        slab_rows.T,
        occ_energy[None, :],
        table,
        singles.T,
        ints,
    )


def grouped_body(amplitudes, singles, pair_list, mirror, slab_rows, occ_energy, vir_energy, integrals):
    owners = lax.axis_size("mem")
    member = lax.axis_index("mem")
    pair_dev = amplitudes.shape[0]
    pair_total = pair_dev * owners
    quarters = lax.all_gather(amplitudes, "grp", axis=1, tiled=True)
    regrouped = lax.all_to_all(quarters, "mem", split_axis=2, concat_axis=0, tiled=True)
    unpacked = regrouped - jnp.take(regrouped, mirror, axis=0)
    group_count = regrouped.shape[1]
    block_len = regrouped.shape[2]
    block_full = block_len * owners
    first_rows = jnp.take(singles, pair_list[:, 0], axis=0)
    second_rows = jnp.take(singles, pair_list[:, 1], axis=0)

    def window(orbital_rows):
        columns = orbital_rows[:, : group_count * block_full].reshape(
            pair_total, group_count, block_full
        )
        return lax.dynamic_slice_in_dim(columns, member * block_len, block_len, 2)

    first_window = window(first_rows)
    second_window = window(second_rows)
    tau_full = (
        unpacked
        + first_window[:, :, :, None] * second_rows[:, None, None, :]
        - second_window[:, :, :, None] * first_rows[:, None, None, :]
    )
    flat_tau = tau_full.reshape(pair_total, -1)
    flat_ints = integrals.reshape(integrals.shape[0], -1)
    summed = lax.psum_scatter(
        0.5
        * lax.dot_general(
            flat_tau,
            flat_ints,
            (((1,), (1,)), ((), ())),
            precision=lax.Precision.HIGHEST,
            preferred_element_type=jnp.float32,
        ),
        "mem",
        scatter_dimension=0,
        tiled=True,
    )
    own_pairs = lax.dynamic_slice_in_dim(pair_list, member * pair_dev, pair_dev, 0)
    occ_first = jnp.take(occ_energy, own_pairs[:, 0])
    occ_second = jnp.take(occ_energy, own_pairs[:, 1])
    vir_first = jnp.take(vir_energy, slab_rows[:, 0])
    vir_second = jnp.take(vir_energy, slab_rows[:, 1])
    denominator = (
        vir_first[None, :] + vir_second[None, :] - occ_first[:, None] - occ_second[:, None]
    )
    return summed / denominator


def solution(mesh):
    owners = mesh.shape["mem"]
    body = grouped_body
    if mesh.shape["grp"] == 1 and owners % (2 * PLANE * CORES) == 0:
        body = functools.partial(kernel_body, owners)
    in_specs = (
        P("mem", "grp", None, None),
        P(),
        P(),
        P(),
        P("grp", None),
        P(),
        P(),
        P("grp", None, "mem", None),
    )
    out_specs = P("mem", "grp")
    return jax.shard_map(body, mesh=mesh, in_specs=in_specs, out_specs=out_specs, check_vma=False)
```

```python
import functools

import jax
import jax.numpy as jnp
from jax import lax
from jax.experimental import pallas as pl
from jax.experimental.pallas import tpu as pltpu
from jax.sharding import PartitionSpec as P

F32 = jnp.float32
BF16 = jnp.bfloat16
LANES = 128
CHUNKS = 2
COLUMN_BLOCKS = 4
PLANE = 4
CORES = 2


def to(device):
    return dict(device_id={"mem": device}, device_id_type=pl.DeviceIdType.MESH)


def bf16_dot(left, right):
    return jnp.dot(left, right, preferred_element_type=F32)


def split_two(value):
    high = value.astype(BF16)
    return high, (value - high.astype(F32)).astype(BF16)


def ladder_kernel(
    n,
    amp_ref,
    mirror_ref,
    pair_ref,
    slab_ref,
    occ_ref,
    vir_ref,
    singles_hbm,
    ints_hbm,
    out_ref,
    send,
    recv,
    singles_ref,
    ints_raw,
    ints_high,
    ints_low,
    spart,
    rows_ref,
    partial,
    got_core,
    got_plane,
    ready_depth,
    got_depth,
    denom_ref,
    table_ref,
    local_sem,
    ints_sem,
    a2a_send,
    a2a_recv,
    core_send,
    core_recv,
    plane_send,
    plane_recv,
    depth_send,
    depth_recv,
):
    me = lax.axis_index("mem")
    pair_dev, _, nc, nv = amp_ref.shape
    pairs = pair_dev * n
    depth_n = n // (PLANE * CORES)
    slab = ints_raw.shape[1]
    width = slab // COLUMN_BLOCKS
    blocks = send.shape[1] // (n * pair_dev)
    per_copy = pair_dev * blocks
    chunk_d = blocks * LANES
    core = lax.rem(me, CORES)
    plane = lax.rem(me // CORES, PLANE)
    depth = me // (CORES * PLANE)

    barrier = pltpu.get_barrier_semaphore()

    @pl.loop(1, n)
    def _(step):
        pl.semaphore_signal(barrier, inc=1, **to(lax.rem(me + step, n)))

    load_singles = pltpu.make_async_copy(singles_hbm, singles_ref, local_sem.at[0])
    load_singles.start()
    piece = nv // ints_sem.shape[0]
    load_ints = []
    for b in range(ints_sem.shape[0]):
        rows = pl.ds(b * piece, piece)
        load_ints.append(
            pltpu.make_async_copy(ints_hbm.at[rows], ints_raw.at[rows], ints_sem.at[b])
        )
        load_ints[-1].start()

    def fill(chunk):
        for j in range(blocks):
            first = (chunk * blocks + j) * LANES
            have = min(LANES, nv - first)
            for p in range(pair_dev):
                if have > 0:
                    value = amp_ref[p, 0, :, first : first + have]
                    if have < LANES:
                        value = jnp.concatenate(
                            [value, jnp.zeros((nc, LANES - have), F32)], axis=1
                        )
                else:
                    value = jnp.zeros((nc, LANES), F32)
                send[chunk, pl.ds(p * blocks + j, nc, stride=per_copy), :] = value

    def block_copy(chunk, target):
        source = pl.ds(pl.multiple_of(target * per_copy, 8), per_copy)
        landing = pl.ds(pl.multiple_of(me * per_copy, 8), per_copy)
        return pltpu.make_async_remote_copy(
            src_ref=send.at[chunk, source],
            dst_ref=recv.at[chunk, landing],
            send_sem=a2a_send.at[chunk],
            recv_sem=a2a_recv.at[chunk],
            **to(target),
        )

    def start_chunk(chunk):
        @pl.loop(1, n)
        def _(step):
            block_copy(chunk, lax.rem(me + step, n)).start()

        mine = pl.ds(pl.multiple_of(me * per_copy, 8), per_copy)
        pltpu.make_async_copy(
            send.at[chunk, mine], recv.at[chunk, mine], a2a_recv.at[chunk]
        ).start()

    fill(0)
    pl.semaphore_wait(barrier, n - 1)
    start_chunk(0)
    for chunk in range(1, CHUNKS):
        fill(chunk)
        start_chunk(chunk)

    table_rows = table_ref.shape[0]
    table_ref[...] = jnp.zeros_like(table_ref)
    energies = vir_ref[...].reshape(1, nv)
    for r in range(table_rows):
        have = min(LANES, nv - r * LANES)
        table_ref[r : r + 1, :have] = energies[:, r * LANES : r * LANES + have]

    def vir_of(which):
        orbital = slab_ref[pl.ds(which, 1), :]
        lane = jnp.bitwise_and(orbital, LANES - 1)
        row = jnp.right_shift(orbital, 7)
        hot = (lax.broadcasted_iota(jnp.int32, (LANES, slab), 0) == lane).astype(F32)
        table = jnp.dot(
            table_ref[...], hot, precision=lax.Precision.HIGHEST, preferred_element_type=F32
        )
        at_row = lax.broadcasted_iota(jnp.int32, (table_rows, slab), 0) == row
        return jnp.sum(jnp.where(at_row, table, 0.0), axis=0, keepdims=True)

    no = occ_ref.shape[0]
    occ = occ_ref[...].reshape(1, no)
    orbitals = pair_ref[...].astype(F32)
    own_hot = lax.broadcasted_iota(jnp.int32, (pair_dev, pairs), 1) == (
        lax.broadcasted_iota(jnp.int32, (pair_dev, pairs), 0) + me * pair_dev
    )
    own_iota = lax.broadcasted_iota(jnp.int32, (pair_dev, no), 1).astype(F32)

    def pick(hot, row):
        return jnp.sum(jnp.where(hot, row, 0.0), axis=1, keepdims=True)


    def occ_of(which):
        return pick(own_iota == pick(own_hot, orbitals[which : which + 1]), occ)

    denom_ref[...] = vir_of(0) + vir_of(1) - occ_of(0) - occ_of(1)

    pair_row = lax.broadcasted_iota(jnp.int32, (pairs, pairs), 0)
    slot = lax.rem(pair_row, pair_dev)
    rest = pair_row // pair_dev
    at_depth = lax.rem(rest, depth_n)
    rest = rest // depth_n
    pair_of_row = (at_depth * PLANE * CORES + lax.rem(rest, PLANE) * CORES + rest // PLANE) * pair_dev + slot
    pair_column = lax.broadcasted_iota(jnp.int32, (pairs, pairs), 1)
    in_order = pair_column == pair_of_row
    partner = pick(in_order, mirror_ref[...].reshape(1, pairs).astype(F32))
    unpack = (
        in_order.astype(F32) - (pair_column.astype(F32) == partner).astype(F32)
    ).astype(BF16)

    load_singles.wait()
    column = singles_ref[pl.ds(me, 1), :]
    pair_iota = lax.broadcasted_iota(jnp.int32, (pairs, no), 1).astype(F32)
    hot_i = pair_iota == pick(in_order, orbitals[0:1])
    hot_j = pair_iota == pick(in_order, orbitals[1:2])
    first_window = pick(hot_i, column)
    second_window = pick(hot_j, column)
    weights = jnp.where(hot_j, first_window, 0.0) - jnp.where(hot_i, second_window, 0.0)
    for chunk in range(CHUNKS):
        first = chunk * chunk_d
        have = min(chunk_d, nv - first)
        value = lax.dot_general(
            weights,
            singles_ref[first : first + have, :],
            (((1,), (1,)), ((), ())),
            precision=lax.Precision.HIGHEST,
            preferred_element_type=F32,
        )
        if have < chunk_d:
            value = jnp.concatenate([value, jnp.zeros((pairs, chunk_d - have), F32)], axis=1)
        spart[chunk] = value

    for b in range(len(load_ints)):
        load_ints[b].wait()

        @pl.loop(0, piece // 16)
        def _(i):
            at = pl.ds(pl.multiple_of(b * piece + i * 16, 16), 16)
            high, low = split_two(ints_raw[at, :])
            ints_high[at, :] = high
            ints_low[at, :] = low

    padded = CHUNKS * chunk_d
    if padded > nv:
        ints_high[nv:padded, :] = jnp.zeros((padded - nv, slab), BF16)
        ints_low[nv:padded, :] = jnp.zeros((padded - nv, slab), BF16)

    half = pairs // CORES
    plane_rows = half // PLANE

    def tau_parts(chunk):
        whole = recv.at[chunk]
        pltpu.make_async_copy(whole, whole, a2a_recv.at[chunk]).wait()
        for j in range(blocks):
            rows_ref[:, j * LANES : (j + 1) * LANES] = recv[chunk, pl.ds(j, pairs, stride=blocks), :]
        value = rows_ref[...]
        one, two = split_two(value)
        three = (value - one.astype(F32) - two.astype(F32)).astype(BF16)
        tau = (bf16_dot(unpack, one) + bf16_dot(unpack, two)) + bf16_dot(unpack, three)
        return split_two(tau + spart[chunk])

    def product(chunk, parts, nb):
        high, low = parts
        at = pl.ds(chunk * chunk_d, chunk_d)
        columns = pl.ds(nb * width, width)
        right = ints_high[at, columns]
        value = bf16_dot(high, right) + bf16_dot(low, right)
        value = value + bf16_dot(high, ints_low[at, columns])
        return value.reshape(CORES, PLANE, plane_rows, width)

    for chunk in range(CHUNKS - 1):
        parts = tau_parts(chunk)
        for nb in range(COLUMN_BLOCKS):
            value = product(chunk, parts, nb)
            partial[nb] = value if chunk == 0 else partial[nb] + value
    parts = tau_parts(CHUNKS - 1)

    def core_copy(nb):
        return pltpu.make_async_remote_copy(
            src_ref=partial.at[nb, 1 - core],
            dst_ref=got_core.at[nb],
            send_sem=core_send.at[nb],
            recv_sem=core_recv.at[nb],
            **to(me + 1 - 2 * core),
        )

    def plane_copy(nb, step):
        other = lax.rem(plane + step, PLANE)
        return pltpu.make_async_remote_copy(
            src_ref=partial.at[nb, core, other],
            dst_ref=got_plane.at[nb, step - 1],
            send_sem=plane_send.at[nb, step - 1],
            recv_sem=plane_recv.at[nb, step - 1],
            **to((depth * PLANE + other) * CORES + core),
        )

    def depth_copy(nb, step):
        other = lax.rem(depth + step, depth_n)
        return pltpu.make_async_remote_copy(
            src_ref=ready_depth.at[nb, other],
            dst_ref=got_depth.at[nb, step - 1],
            send_sem=depth_send.at[nb, step - 1],
            recv_sem=depth_recv.at[nb, step - 1],
            **to((other * PLANE + plane) * CORES + core),
        )

    def contract(nb):
        value = product(CHUNKS - 1, parts, nb)
        partial[nb] = partial[nb] + value if CHUNKS > 1 else value
        core_copy(nb).start()

    def add_core(nb):
        core_copy(nb).wait_recv()
        partial[nb, core] = partial[nb, core] + got_core[nb]
        for step in range(1, PLANE):
            plane_copy(nb, step).start()

    def add_plane(nb):
        for step in range(1, PLANE):
            plane_copy(nb, step).wait_recv()
        value = partial[nb, core, plane]
        for step in range(1, PLANE):
            value = value + got_plane[nb, step - 1]
        for z in range(depth_n):
            ready_depth[nb, z] = value[z * pair_dev : (z + 1) * pair_dev]
        for step in range(1, depth_n):
            depth_copy(nb, step).start()

    def add_depth(nb):
        for step in range(1, depth_n):
            depth_copy(nb, step).wait_recv()
        value = ready_depth[nb, depth]
        for step in range(1, depth_n):
            value = value + got_depth[nb, step - 1]
        columns = slice(nb * width, (nb + 1) * width)
        out_ref[:, columns] = value / denom_ref[:, columns]

    for step in range(COLUMN_BLOCKS + 3):
        for lag, stage in enumerate((contract, add_core, add_plane, add_depth)):
            if 0 <= step - lag < COLUMN_BLOCKS:
                stage(step - lag)

    for nb in range(COLUMN_BLOCKS):
        core_copy(nb).wait_send()
        for step in range(1, PLANE):
            plane_copy(nb, step).wait_send()
        for step in range(1, depth_n):
            depth_copy(nb, step).wait_send()
    for chunk in range(CHUNKS):
        @pl.loop(1, n)
        def _(step):
            block_copy(chunk, lax.rem(me + step, n)).wait_send()


def kernel_body(n, amplitudes, singles, pair_list, mirror, slab_rows, occ_energy, vir_energy, integrals):
    pair_dev, _, nc, nv = amplitudes.shape
    slab = integrals.shape[0]
    no = singles.shape[0]
    pairs = pair_dev * n
    depth_n = n // (PLANE * CORES)
    blocks = -(-nv // (LANES * CHUNKS))
    padded = blocks * CHUNKS * LANES
    width = slab // COLUMN_BLOCKS

    ints = jnp.transpose(integrals, (1, 2, 3, 0)).reshape(nv, slab)
    pieces = max(k for k in range(1, 9) if nv % (16 * k) == 0)
    vmem = pl.BlockSpec(memory_space=pltpu.VMEM)
    hbm = pl.BlockSpec(memory_space=pl.ANY)
    dma = pltpu.SemaphoreType.DMA
    plane_rows = pairs // (CORES * PLANE)
    scaled = pl.pallas_call(
        functools.partial(ladder_kernel, n),
        out_shape=jax.ShapeDtypeStruct((pair_dev, slab), F32),
        in_specs=[vmem] * 6 + [hbm] * 2,
        out_specs=vmem,
        scratch_shapes=[
            pltpu.VMEM((CHUNKS, pairs * blocks, LANES), F32),
            pltpu.VMEM((CHUNKS, pairs * blocks, LANES), F32),
            pltpu.VMEM((nv, no), F32),
            pltpu.VMEM((nv, slab), F32),
            pltpu.VMEM((padded, slab), BF16),
            pltpu.VMEM((padded, slab), BF16),
            pltpu.VMEM((CHUNKS, pairs, blocks * LANES), F32),
            pltpu.VMEM((pairs, blocks * LANES), F32),
            pltpu.VMEM((COLUMN_BLOCKS, CORES, PLANE, plane_rows, width), F32),
            pltpu.VMEM((COLUMN_BLOCKS, PLANE, plane_rows, width), F32),
            pltpu.VMEM((COLUMN_BLOCKS, PLANE - 1, plane_rows, width), F32),
            pltpu.VMEM((COLUMN_BLOCKS, depth_n, pair_dev, width), F32),
            pltpu.VMEM((COLUMN_BLOCKS, depth_n - 1, pair_dev, width), F32),
            pltpu.VMEM((pair_dev, slab), F32),
            pltpu.VMEM((-(-nv // LANES), LANES), F32),
            dma((1,)),
            dma((pieces,)),
            dma((CHUNKS,)),
            dma((CHUNKS,)),
            dma((COLUMN_BLOCKS,)),
            dma((COLUMN_BLOCKS,)),
            dma((COLUMN_BLOCKS, PLANE - 1)),
            dma((COLUMN_BLOCKS, PLANE - 1)),
            dma((COLUMN_BLOCKS, depth_n - 1)),
            dma((COLUMN_BLOCKS, depth_n - 1)),
        ],
        compiler_params=pltpu.CompilerParams(
            collective_id=0, has_side_effects=True, vmem_limit_bytes=58 * 2**20
        ),
    )(
        amplitudes,
        mirror,
        pair_list.T,
        slab_rows.T,
        occ_energy,
        vir_energy,
        singles.T,
        ints,
    )
    return 0.5 * scaled


def grouped_body(amplitudes, singles, pair_list, mirror, slab_rows, occ_energy, vir_energy, integrals):
    owners = lax.axis_size("mem")
    member = lax.axis_index("mem")
    pair_dev = amplitudes.shape[0]
    pair_total = pair_dev * owners
    quarters = lax.all_gather(amplitudes, "grp", axis=1, tiled=True)
    regrouped = lax.all_to_all(quarters, "mem", split_axis=2, concat_axis=0, tiled=True)
    unpacked = regrouped - jnp.take(regrouped, mirror, axis=0)
    group_count = regrouped.shape[1]
    block_len = regrouped.shape[2]
    block_full = block_len * owners
    first_rows = jnp.take(singles, pair_list[:, 0], axis=0)
    second_rows = jnp.take(singles, pair_list[:, 1], axis=0)

    def window(orbital_rows):
        columns = orbital_rows[:, : group_count * block_full].reshape(
            pair_total, group_count, block_full
        )
        return lax.dynamic_slice_in_dim(columns, member * block_len, block_len, 2)

    first_window = window(first_rows)
    second_window = window(second_rows)
    tau_full = (
        unpacked
        + first_window[:, :, :, None] * second_rows[:, None, None, :]
        - second_window[:, :, :, None] * first_rows[:, None, None, :]
    )
    flat_tau = tau_full.reshape(pair_total, -1)
    flat_ints = integrals.reshape(integrals.shape[0], -1)
    summed = lax.psum_scatter(
        0.5
        * lax.dot_general(
            flat_tau,
            flat_ints,
            (((1,), (1,)), ((), ())),
            precision=lax.Precision.HIGHEST,
            preferred_element_type=jnp.float32,
        ),
        "mem",
        scatter_dimension=0,
        tiled=True,
    )
    own_pairs = lax.dynamic_slice_in_dim(pair_list, member * pair_dev, pair_dev, 0)
    occ_first = jnp.take(occ_energy, own_pairs[:, 0])
    occ_second = jnp.take(occ_energy, own_pairs[:, 1])
    vir_first = jnp.take(vir_energy, slab_rows[:, 0])
    vir_second = jnp.take(vir_energy, slab_rows[:, 1])
    denominator = (
        vir_first[None, :] + vir_second[None, :] - occ_first[:, None] - occ_second[:, None]
    )
    return summed / denominator


def solution(mesh):
    owners = mesh.shape["mem"]
    body = grouped_body
    if mesh.shape["grp"] == 1 and owners % (2 * PLANE * CORES) == 0:
        body = functools.partial(kernel_body, owners)
    in_specs = (
        P("mem", "grp", None, None),
        P(),
        P(),
        P(),
        P("grp", None),
        P(),
        P(),
        P("grp", None, "mem", None),
    )
    out_specs = P("mem", "grp")
    return jax.shard_map(body, mesh=mesh, in_specs=in_specs, out_specs=out_specs, check_vma=False)
```

```python
import functools

import jax
import jax.numpy as jnp
from jax import lax
from jax.experimental import pallas as pl
from jax.experimental.pallas import tpu as pltpu
from jax.sharding import PartitionSpec as P

F32 = jnp.float32
BF16 = jnp.bfloat16
LANES = 128
COLUMN_BLOCKS = 4
PLANE = 4
CORES = 2


def to(device):
    return dict(device_id={"mem": device}, device_id_type=pl.DeviceIdType.MESH)


def bf16_dot(left, right):
    return jnp.dot(left, right, preferred_element_type=F32)


def split_two(value):
    high = value.astype(BF16)
    return high, (value - high.astype(F32)).astype(BF16)


def ladder_kernel(
    n,
    amp_ref,
    mirror_ref,
    pair_ref,
    slab_ref,
    occ_ref,
    vir_ref,
    singles_hbm,
    ints_hbm,
    out_ref,
    send,
    recv,
    singles_ref,
    ints_raw,
    ints_high,
    ints_low,
    spart,
    rows_ref,
    partial,
    got_core,
    got_plane,
    ready_depth,
    got_depth,
    denom_ref,
    table_ref,
    local_sem,
    ints_sem,
    a2a_send,
    a2a_recv,
    core_send,
    core_recv,
    plane_send,
    plane_recv,
    depth_send,
    depth_recv,
):
    me = lax.axis_index("mem")
    pair_dev, _, nc, nv = amp_ref.shape
    pairs = pair_dev * n
    depth_n = n // (PLANE * CORES)
    slab = ints_raw.shape[1]
    width = slab // COLUMN_BLOCKS
    blocks = -(-nv // LANES)
    per_copy = pair_dev * blocks
    padded = blocks * LANES
    half = pairs // CORES
    plane_rows = half // PLANE
    core = lax.rem(me, CORES)
    plane = lax.rem(me // CORES, PLANE)
    depth = me // (CORES * PLANE)

    barrier = pltpu.get_barrier_semaphore()

    @pl.loop(1, n)
    def _(step):
        pl.semaphore_signal(barrier, inc=1, **to(lax.rem(me + step, n)))

    load_singles = pltpu.make_async_copy(singles_hbm, singles_ref, local_sem.at[0])
    load_singles.start()
    piece = nv // ints_sem.shape[0]
    load_ints = []
    for b in range(ints_sem.shape[0]):
        rows = pl.ds(b * piece, piece)
        load_ints.append(
            pltpu.make_async_copy(ints_hbm.at[rows], ints_raw.at[rows], ints_sem.at[b])
        )
        load_ints[-1].start()

    for j in range(blocks):
        first = j * LANES
        have = min(LANES, nv - first)
        for p in range(pair_dev):
            value = amp_ref[p, 0, :, first : first + have]
            if have < LANES:
                value = jnp.concatenate([value, jnp.zeros((nc, LANES - have), F32)], axis=1)
            send[pl.ds(p * blocks + j, nc, stride=per_copy), :] = value

    landing = pl.ds(pl.multiple_of((me // CORES) * per_copy, 8), per_copy)

    def block_copy(target):
        source = pl.ds(pl.multiple_of(target * per_copy, 8), per_copy)
        return pltpu.make_async_remote_copy(
            src_ref=send.at[source],
            dst_ref=recv.at[core, landing],
            send_sem=a2a_send.at[0],
            recv_sem=a2a_recv.at[core],
            **to(target),
        )

    def start_blocks():
        @pl.loop(1, n)
        def _(step):
            block_copy(lax.rem(me + step, n)).start()

        mine = pl.ds(pl.multiple_of(me * per_copy, 8), per_copy)
        pltpu.make_async_copy(
            send.at[mine], recv.at[core, landing], a2a_recv.at[core]
        ).start()

    pl.semaphore_wait(barrier, n - 1)

    @pl.when(core == 0)
    def _():
        start_blocks()

    table_rows = table_ref.shape[0]
    table_ref[...] = jnp.zeros_like(table_ref)
    energies = vir_ref[...].reshape(1, nv)
    for r in range(table_rows):
        have = min(LANES, nv - r * LANES)
        table_ref[r : r + 1, :have] = energies[:, r * LANES : r * LANES + have]

    def vir_of(which):
        orbital = slab_ref[pl.ds(which, 1), :]
        lane = jnp.bitwise_and(orbital, LANES - 1)
        row = jnp.right_shift(orbital, 7)
        hot = (lax.broadcasted_iota(jnp.int32, (LANES, slab), 0) == lane).astype(F32)
        table = jnp.dot(
            table_ref[...], hot, precision=lax.Precision.HIGHEST, preferred_element_type=F32
        )
        at_row = lax.broadcasted_iota(jnp.int32, (table_rows, slab), 0) == row
        return jnp.sum(jnp.where(at_row, table, 0.0), axis=0, keepdims=True)

    no = occ_ref.shape[0]
    occ = occ_ref[...].reshape(1, no)
    orbitals = pair_ref[...].astype(F32)
    own_hot = lax.broadcasted_iota(jnp.int32, (pair_dev, pairs), 1) == (
        lax.broadcasted_iota(jnp.int32, (pair_dev, pairs), 0) + me * pair_dev
    )
    own_iota = lax.broadcasted_iota(jnp.int32, (pair_dev, no), 1).astype(F32)

    def pick(hot, row):
        return jnp.sum(jnp.where(hot, row, 0.0), axis=1, keepdims=True)


    def occ_of(which):
        return pick(own_iota == pick(own_hot, orbitals[which : which + 1]), occ)

    denom_ref[...] = vir_of(0) + vir_of(1) - occ_of(0) - occ_of(1)

    pair_row = lax.broadcasted_iota(jnp.int32, (pairs, pairs), 0)
    slot = lax.rem(pair_row, pair_dev)
    rest = pair_row // pair_dev
    at_depth = lax.rem(rest, depth_n)
    rest = rest // depth_n
    pair_of_row = (at_depth * PLANE * CORES + lax.rem(rest, PLANE) * CORES + rest // PLANE) * pair_dev + slot
    pair_column = lax.broadcasted_iota(jnp.int32, (pairs, pairs), 1)
    in_order = pair_column == pair_of_row
    partner = pick(in_order, mirror_ref[...].reshape(1, pairs).astype(F32))
    group_column = lax.broadcasted_iota(jnp.int32, (half, half), 1)

    def unpack_of(group):
        pair_here = (group_column // pair_dev * CORES + group) * pair_dev + lax.rem(
            group_column, pair_dev
        )
        rows = slice(group * half, (group + 1) * half)
        same = pair_here == pair_of_row[rows, :half]
        mirrored = pair_here.astype(F32) == partner[rows]
        return (same.astype(F32) - mirrored.astype(F32)).astype(BF16)

    load_singles.wait()
    column = singles_ref[pl.ds(me, 1), :]
    pair_iota = lax.broadcasted_iota(jnp.int32, (pairs, no), 1).astype(F32)
    hot_i = pair_iota == pick(in_order, orbitals[0:1])
    hot_j = pair_iota == pick(in_order, orbitals[1:2])
    first_window = pick(hot_i, column)
    second_window = pick(hot_j, column)
    weights = jnp.where(hot_j, first_window, 0.0) - jnp.where(hot_i, second_window, 0.0)
    singles_part = lax.dot_general(
        weights,
        singles_ref[...],
        (((1,), (1,)), ((), ())),
        precision=lax.Precision.HIGHEST,
        preferred_element_type=F32,
    )
    if padded > nv:
        singles_part = jnp.concatenate(
            [singles_part, jnp.zeros((pairs, padded - nv), F32)], axis=1
        )
    for group in range(CORES):
        spart[group] = singles_part[group * half : (group + 1) * half]

    for b in range(len(load_ints)):
        load_ints[b].wait()

        @pl.loop(0, piece // 16)
        def _(i):
            at = pl.ds(pl.multiple_of(b * piece + i * 16, 16), 16)
            high, low = split_two(ints_raw[at, :])
            ints_high[at, :] = high
            ints_low[at, :] = low

    if padded > nv:
        ints_high[nv:padded, :] = jnp.zeros((padded - nv, slab), BF16)
        ints_low[nv:padded, :] = jnp.zeros((padded - nv, slab), BF16)

    def wait_group(group):
        whole = recv.at[group]
        pltpu.make_async_copy(whole, whole, a2a_recv.at[group]).wait()

    def tau_parts(group):
        for j in range(blocks):
            rows_ref[:, j * LANES : (j + 1) * LANES] = recv[group, pl.ds(j, half, stride=blocks), :]
        value = rows_ref[...]
        one, two = split_two(value)
        three = (value - one.astype(F32) - two.astype(F32)).astype(BF16)
        unpack = unpack_of(group)
        tau = (bf16_dot(unpack, one) + bf16_dot(unpack, two)) + bf16_dot(unpack, three)
        return split_two(tau + spart[group])

    def core_copy(group, nb):
        return pltpu.make_async_remote_copy(
            src_ref=partial.at[group, nb],
            dst_ref=got_core.at[nb],
            send_sem=core_send.at[nb],
            recv_sem=core_recv.at[nb],
            **to(me + 1 - 2 * core),
        )

    def plane_copy(group, nb, step):
        other = lax.rem(plane + step, PLANE)
        return pltpu.make_async_remote_copy(
            src_ref=partial.at[group, nb, other],
            dst_ref=got_plane.at[nb, step - 1],
            send_sem=plane_send.at[nb, step - 1],
            recv_sem=plane_recv.at[nb, step - 1],
            **to((depth * PLANE + other) * CORES + core),
        )

    def depth_copy(nb, step):
        other = lax.rem(depth + step, depth_n)
        return pltpu.make_async_remote_copy(
            src_ref=ready_depth.at[nb, other],
            dst_ref=got_depth.at[nb, step - 1],
            send_sem=depth_send.at[nb, step - 1],
            recv_sem=depth_recv.at[nb, step - 1],
            **to((other * PLANE + plane) * CORES + core),
        )

    def contract(group, parts, nb):
        high, low = parts
        columns = pl.ds(nb * width, width)
        right = ints_high[:, columns]
        value = bf16_dot(high, right) + bf16_dot(low, right)
        value = value + bf16_dot(high, ints_low[:, columns])
        partial[group, nb] = value.reshape(PLANE, plane_rows, width)

        @pl.when(core != group)
        def _():
            core_copy(group, nb).start()

    def add_core(group, nb):
        core_copy(group, nb).wait_recv()
        partial[group, nb] = partial[group, nb] + got_core[nb]
        for step in range(1, PLANE):
            plane_copy(group, nb, step).start()

    def add_plane(group, nb):
        for step in range(1, PLANE):
            plane_copy(group, nb, step).wait_recv()
        value = partial[group, nb, plane]
        for step in range(1, PLANE):
            value = value + got_plane[nb, step - 1]
        for z in range(depth_n):
            ready_depth[nb, z] = value[z * pair_dev : (z + 1) * pair_dev]
        for step in range(1, depth_n):
            depth_copy(nb, step).start()

    def add_depth(group, nb):
        for step in range(1, depth_n):
            depth_copy(nb, step).wait_recv()
        value = ready_depth[nb, depth]
        for step in range(1, depth_n):
            value = value + got_depth[nb, step - 1]
        columns = slice(nb * width, (nb + 1) * width)
        out_ref[:, columns] = value / denom_ref[:, columns]

    for group in range(CORES):
        wait_group(group)
        if group == 0:
            @pl.when(core == 1)
            def _():
                start_blocks()

        parts = tau_parts(group)
        for step in range(COLUMN_BLOCKS + 3):
            if step < COLUMN_BLOCKS:
                contract(group, parts, step)

            @pl.when(core == group)
            def _():
                for lag, stage in enumerate((add_core, add_plane, add_depth)):
                    if 0 <= step - lag - 1 < COLUMN_BLOCKS:
                        stage(group, step - lag - 1)

    for nb in range(COLUMN_BLOCKS):
        core_copy(0, nb).wait_send()
        for step in range(1, PLANE):
            plane_copy(0, nb, step).wait_send()
        for step in range(1, depth_n):
            depth_copy(nb, step).wait_send()

    @pl.loop(1, n)
    def _(step):
        block_copy(lax.rem(me + step, n)).wait_send()


def kernel_body(n, amplitudes, singles, pair_list, mirror, slab_rows, occ_energy, vir_energy, integrals):
    pair_dev, _, nc, nv = amplitudes.shape
    slab = integrals.shape[0]
    no = singles.shape[0]
    pairs = pair_dev * n
    depth_n = n // (PLANE * CORES)
    blocks = -(-nv // LANES)
    padded = blocks * LANES
    half = pairs // CORES
    width = slab // COLUMN_BLOCKS

    ints = jnp.transpose(integrals, (1, 2, 3, 0)).reshape(nv, slab)
    pieces = max(k for k in range(1, 9) if nv % (16 * k) == 0)
    vmem = pl.BlockSpec(memory_space=pltpu.VMEM)
    hbm = pl.BlockSpec(memory_space=pl.ANY)
    dma = pltpu.SemaphoreType.DMA
    plane_rows = pairs // (CORES * PLANE)
    scaled = pl.pallas_call(
        functools.partial(ladder_kernel, n),
        out_shape=jax.ShapeDtypeStruct((pair_dev, slab), F32),
        in_specs=[vmem] * 6 + [hbm] * 2,
        out_specs=vmem,
        scratch_shapes=[
            pltpu.VMEM((nc * pair_dev * blocks, LANES), F32),
            pltpu.VMEM((CORES, half * blocks, LANES), F32),
            pltpu.VMEM((nv, no), F32),
            pltpu.VMEM((nv, slab), F32),
            pltpu.VMEM((padded, slab), BF16),
            pltpu.VMEM((padded, slab), BF16),
            pltpu.VMEM((CORES, half, padded), F32),
            pltpu.VMEM((half, padded), F32),
            pltpu.VMEM((CORES, COLUMN_BLOCKS, PLANE, plane_rows, width), F32),
            pltpu.VMEM((COLUMN_BLOCKS, PLANE, plane_rows, width), F32),
            pltpu.VMEM((COLUMN_BLOCKS, PLANE - 1, plane_rows, width), F32),
            pltpu.VMEM((COLUMN_BLOCKS, depth_n, pair_dev, width), F32),
            pltpu.VMEM((COLUMN_BLOCKS, depth_n - 1, pair_dev, width), F32),
            pltpu.VMEM((pair_dev, slab), F32),
            pltpu.VMEM((-(-nv // LANES), LANES), F32),
            dma((1,)),
            dma((pieces,)),
            dma((1,)),
            dma((CORES,)),
            dma((COLUMN_BLOCKS,)),
            dma((COLUMN_BLOCKS,)),
            dma((COLUMN_BLOCKS, PLANE - 1)),
            dma((COLUMN_BLOCKS, PLANE - 1)),
            dma((COLUMN_BLOCKS, depth_n - 1)),
            dma((COLUMN_BLOCKS, depth_n - 1)),
        ],
        compiler_params=pltpu.CompilerParams(
            collective_id=0, has_side_effects=True, vmem_limit_bytes=58 * 2**20
        ),
    )(
        amplitudes,
        mirror,
        pair_list.T,
        slab_rows.T,
        occ_energy,
        vir_energy,
        singles.T,
        ints,
    )
    return 0.5 * scaled


def grouped_body(amplitudes, singles, pair_list, mirror, slab_rows, occ_energy, vir_energy, integrals):
    owners = lax.axis_size("mem")
    member = lax.axis_index("mem")
    pair_dev = amplitudes.shape[0]
    pair_total = pair_dev * owners
    quarters = lax.all_gather(amplitudes, "grp", axis=1, tiled=True)
    regrouped = lax.all_to_all(quarters, "mem", split_axis=2, concat_axis=0, tiled=True)
    unpacked = regrouped - jnp.take(regrouped, mirror, axis=0)
    group_count = regrouped.shape[1]
    block_len = regrouped.shape[2]
    block_full = block_len * owners
    first_rows = jnp.take(singles, pair_list[:, 0], axis=0)
    second_rows = jnp.take(singles, pair_list[:, 1], axis=0)

    def window(orbital_rows):
        columns = orbital_rows[:, : group_count * block_full].reshape(
            pair_total, group_count, block_full
        )
        return lax.dynamic_slice_in_dim(columns, member * block_len, block_len, 2)

    first_window = window(first_rows)
    second_window = window(second_rows)
    tau_full = (
        unpacked
        + first_window[:, :, :, None] * second_rows[:, None, None, :]
        - second_window[:, :, :, None] * first_rows[:, None, None, :]
    )
    flat_tau = tau_full.reshape(pair_total, -1)
    flat_ints = integrals.reshape(integrals.shape[0], -1)
    summed = lax.psum_scatter(
        0.5
        * lax.dot_general(
            flat_tau,
            flat_ints,
            (((1,), (1,)), ((), ())),
            precision=lax.Precision.HIGHEST,
            preferred_element_type=jnp.float32,
        ),
        "mem",
        scatter_dimension=0,
        tiled=True,
    )
    own_pairs = lax.dynamic_slice_in_dim(pair_list, member * pair_dev, pair_dev, 0)
    occ_first = jnp.take(occ_energy, own_pairs[:, 0])
    occ_second = jnp.take(occ_energy, own_pairs[:, 1])
    vir_first = jnp.take(vir_energy, slab_rows[:, 0])
    vir_second = jnp.take(vir_energy, slab_rows[:, 1])
    denominator = (
        vir_first[None, :] + vir_second[None, :] - occ_first[:, None] - occ_second[:, None]
    )
    return summed / denominator


def solution(mesh):
    owners = mesh.shape["mem"]
    body = grouped_body
    if mesh.shape["grp"] == 1 and owners % (2 * PLANE * CORES) == 0:
        body = functools.partial(kernel_body, owners)
    in_specs = (
        P("mem", "grp", None, None),
        P(),
        P(),
        P(),
        P("grp", None),
        P(),
        P(),
        P("grp", None, "mem", None),
    )
    out_specs = P("mem", "grp")
    return jax.shard_map(body, mesh=mesh, in_specs=in_specs, out_specs=out_specs, check_vma=False)
```
